768 devices in a mesh: dom: 192 (over y, z, core), help: 4 (over x).
Axes of the slice: x: 4, y: 8, z: 12, core: 2. Of those that a mesh axis runs over, the one named last changes fastest.
Arguments:
- features: bfloat16 [196608, 256], P(('dom', 'help')), may hold values from -6 to 6
- tile_vals: bfloat16 [36864, 128, 128], P(('dom', 'help')), as said below
- tile_dst: int32 [36864], P(('dom', 'help')), may hold values from 0 to 7
- tile_src: int32 [36864], P(('dom', 'help')), may hold values from 0 to 39
- w_self: bfloat16 [256, 256], replicated, may hold values from -0.375 to 0.375
- w_neigh: bfloat16 [256, 256], replicated, may hold values from -0.375 to 0.375
- cotangent: bfloat16 [196608, 256], P(('dom', 'help')), may hold values from -6 to 6
Outputs:
- hidden_out: bfloat16 [196608, 256], P(('dom', 'help'))
- grad_features: float32 [196608, 256], P(('dom', 'help'))
- grad_self: float32 [256, 256], replicated
- grad_neigh: float32 [256, 256], replicated
The draws below stay inside these ranges and needn't reach their ends.
Inputs may be any that keep to these rules, and one draw needn't show every extreme that they name: `tile_vals`: edge weights are non-negative.
All inputs are finite; a program needn't handle non-finite values.
Results may differ from the reference program's by a relative error of at most 0.013.
Values may be sent and summed in bfloat16 or wider, within the bound.
A program may use at most 64 MiB of HBM per device.

```python
import math
import jax
import jax.numpy as jnp
import numpy as np
from jax import lax

F = 256
BLOCK = 128
BLK_DEV = 2
TILE_BLK = 24
RADIUS = 2
TILE_DEV = 48
PART_BLK = 8
BAND_BLK = 40
NODES = 196608
TILES = 36864
N_DOM = 192
N_HELP = 4


def draw_tile_vals(key, part):
    key = jax.random.fold_in(key, 11)
    keep_key, size_key = jax.random.split(key)
    shape = (TILES, BLOCK, BLOCK)
    keep = (jax.random.uniform(keep_key, shape, jnp.float32) < 0.4).astype(jnp.float32)
    magnitude = jax.random.uniform(size_key, shape, jnp.float32, 0.0, 1.0)
    factor = 2.7 / math.sqrt(BLOCK * TILE_BLK)
    return (keep * magnitude * factor).astype(jnp.bfloat16)


def plant(drawn, stream_key, low, top_value):
    longest = drawn.shape.index(max(drawn.shape))
    spots = []
    for shift in (0, 1):
        where = [jax.random.randint(jax.random.fold_in(stream_key, axis), (), 0, length) for axis, length in enumerate(drawn.shape)]
        where[longest] = (where[longest] + shift) % drawn.shape[longest]
        spots.append(tuple(where))
    return drawn.at[spots[0]].set(low).at[spots[1]].set(top_value)


def levels(key, shape, cuts, least, largest):
    def one(dim, shards_of):
        draws = jax.random.uniform(jax.random.fold_in(jax.random.fold_in(key, 6), dim), (shards_of,), jnp.float32, least / len(cuts), largest / len(cuts))
        return jnp.repeat(jnp.exp(draws), shape[dim] // shards_of).reshape((-1,) + (1,) * (len(shape) - dim - 1))

    level = one(*cuts[0])
    for cut in cuts[1:]:
        level = level * one(*cut)
    return level


def rank_table(amount, skew):
    loads = [(1 << 20) // math.isqrt(standing ** skew) + 1 for standing in range(1, amount + 1)]
    scale = 1 + sum(loads) // (1 << 30)
    return np.cumsum(np.array([max(1, weight // scale) for weight in loads]))


def ranked_ids(rng, extent, count, lean):
    grid = rank_table(count, lean)
    lot = jax.random.randint(jax.random.fold_in(rng, 1), extent, 0, int(grid[count - 1]))
    rank = jnp.searchsorted(jnp.asarray(grid, jnp.int32), lot, side="right")
    return jax.random.permutation(jax.random.fold_in(rng, 2), count)[rank].astype(jnp.int32)


def gaussian(rng, extent, width, limit, cuts=(), held_as=jnp.bfloat16):
    drawn = width * jax.random.normal(rng, extent, jnp.float32)
    if cuts:
        drawn = drawn * levels(rng, extent, cuts, -0.22, 0.18)
    return jnp.clip(drawn, -limit, limit).astype(held_as)


def setup_inputs(seed: int = 0) -> dict:
    streams_of = jax.random.split(jax.random.key(seed), 8)
    return {
        "features": gaussian(streams_of[0], (NODES, F), 1.0, 6.0, ((0, 768),)),
        "tile_vals": draw_tile_vals(jax.random.fold_in(streams_of[7], 71), 0),
        "tile_dst": plant(ranked_ids(streams_of[2], (TILES,), PART_BLK, 2), jax.random.fold_in(streams_of[2], 3), 0, PART_BLK - 1).astype(jnp.int32),
        "tile_src": plant(jax.random.randint(streams_of[3], (TILES,), 0, BAND_BLK), jax.random.fold_in(streams_of[3], 1), 0, BAND_BLK - 1).astype(jnp.int32),
        "w_self": gaussian(streams_of[4], (F, F), F ** -0.5, 0.375),
        "w_neigh": gaussian(streams_of[5], (F, F), F ** -0.5, 0.375),
        "cotangent": gaussian(streams_of[6], (NODES, F), 1.0, 6.0, ((0, 768),)),
    }


def reference(features, tile_vals, tile_dst, tile_src, w_self, w_neigh, cotangent):
    part_blocks = BLK_DEV * N_HELP
    band_span = 2 * RADIUS + 1
    band_blocks = band_span * part_blocks
    tiles_part = TILE_DEV * N_HELP
    partitions = features.reshape(N_DOM, part_blocks, BLOCK, F)
    values = tile_vals.reshape(N_DOM, tiles_part, BLOCK, BLOCK)
    dests = tile_dst.reshape(N_DOM, tiles_part)
    sources = tile_src.reshape(N_DOM, tiles_part)
    offsets = jnp.arange(-RADIUS, RADIUS + 1, dtype=jnp.int32)
    dest_range = jnp.arange(part_blocks, dtype=jnp.int32)
    band_range = jnp.arange(band_blocks, dtype=jnp.int32)

    def forward_part(index):
        owners = (index + offsets) % N_DOM
        source_rows = partitions[owners].reshape(band_blocks, BLOCK, F)
        picked = source_rows[sources[index]].astype(jnp.float32)
        products = jnp.einsum("tij,tjf->tif", values[index].astype(jnp.float32), picked)
        onehot = (dests[index][None, :] == dest_range[:, None]).astype(jnp.float32)
        return jnp.einsum("dt,tif->dif", onehot, products, precision=lax.Precision.HIGHEST)

    agg_sum = lax.map(forward_part, jnp.arange(N_DOM, dtype=jnp.int32))
    aggregate = agg_sum.reshape(NODES, F).astype(jnp.bfloat16)
    pre_act = jnp.dot(features, w_self, preferred_element_type=jnp.float32) + jnp.dot(aggregate, w_neigh, preferred_element_type=jnp.float32)
    squash = jax.nn.sigmoid(pre_act)
    hidden_out = (pre_act * squash).astype(jnp.bfloat16)
    slope = squash * (1.0 + pre_act * (1.0 - squash))
    grad_pre = (cotangent.astype(jnp.float32) * slope).astype(jnp.bfloat16)
    grad_self = jnp.dot(features.T, grad_pre, preferred_element_type=jnp.float32)
    grad_neigh = jnp.dot(aggregate.T, grad_pre, preferred_element_type=jnp.float32)
    dest_grad = jnp.dot(grad_pre, w_neigh.T, preferred_element_type=jnp.float32).astype(jnp.bfloat16)
    dest_parts = dest_grad.reshape(N_DOM, part_blocks, BLOCK, F)

    def backward_part(carry, index):
        picked = dest_parts[index][dests[index]].astype(jnp.float32)
        products = jnp.einsum("tji,tjf->tif", values[index].astype(jnp.float32), picked)
        onehot = (sources[index][None, :] == band_range[:, None]).astype(jnp.float32)
        band_terms = jnp.einsum("st,tif->sif", onehot, products, precision=lax.Precision.HIGHEST)
        band_terms = band_terms.reshape(band_span, part_blocks, BLOCK, F)
        for slot in range(band_span):
            owner = (index + slot - RADIUS) % N_DOM
            carry = carry.at[owner].add(band_terms[slot])
        return carry, None

    start = jnp.zeros((N_DOM, part_blocks, BLOCK, F), jnp.float32)
    back, unused = lax.scan(backward_part, start, jnp.arange(N_DOM, dtype=jnp.int32))
    grad_features = jnp.dot(grad_pre, w_self.T, preferred_element_type=jnp.float32) + back.reshape(NODES, F)
    return hidden_out, grad_features, grad_self, grad_neigh
```

```python
import functools

import jax
import jax.numpy as jnp
from jax import lax
from jax.experimental import pallas as pl
from jax.experimental.pallas import tpu as pltpu
from jax.sharding import PartitionSpec as P

MESH = pl.DeviceIdType.MESH
F32, BF16 = jnp.float32, jnp.bfloat16
HELP = 4
Z_SIZE = 12
UNROLL = 16


def kernel(
    n_dom,
    dst_hbm,
    src_hbm,
    feat_hbm,
    tiles_hbm,
    ws_hbm,
    wn_hbm,
    cot_hbm,
    hid_hbm,
    gf_hbm,
    gw_hbm,
    hid_ref,
    gf_ref,
    gw_ref,
    keys,
    feat_ref,
    ws_ref,
    wn_ref,
    cot_ref,
    tiles,
    order_v,
    idx,
    band,
    prods,
    part,
    relay,
    part_in,
    dest,
    mats,
    mats_out,
    ar_sib,
    ar_x,
    ar_xin,
    ar_z,
    ar_fin,
    sib_out,
    sib_in,
    g,
    za_in,
    rb_in,
    fb_in,
    zb_out,
    zb_in,
    ra_in,
    fa_in,
    own_pre,
    send_sem,
    recv_sem,
    local_sem,
    far_sem,
):
    n_y = n_dom // (2 * Z_SIZE)
    n_tiles, blk = tiles.shape[0], tiles.shape[1]
    half = blk // 2
    d, h = lax.axis_index("dom"), lax.axis_index("help")
    c, k = d % 2, d // 2
    z, y = k % Z_SIZE, k // Z_SIZE
    hr, hl, ho = (h + 1) % HELP, (h + 3) % HELP, (h + 2) % HELP

    sib = (d + 1 - 2 * c, h)
    right, left = (d, hr), (d, hl)

    def xy_peer(i, j):
        return ((((y + j) % n_y) * Z_SIZE + z) * 2 + c, (h + i) % HELP)

    znext, zprev = ((d + 2) % n_dom, h), ((d + n_dom - 2) % n_dom, h)
    y_peers = [xy_peer(0, j) for j in range(1, n_y)]
    def hops(steps, size):
        return min(steps, size - steps)

    xy_steps = [(i, j) for i in range(HELP) for j in range(n_y) if i or j]
    xy_steps.sort(key=lambda ij: -hops(ij[0], HELP) - hops(ij[1], n_y))
    z_steps = sorted(range(1, Z_SIZE), key=lambda j: -hops(j, Z_SIZE))
    z_peers = [((y * Z_SIZE + (z + j) % Z_SIZE) * 2 + c, h) for j in range(1, Z_SIZE)]

    barrier = pltpu.get_barrier_semaphore()
    near = [sib, right, left, znext, zprev, z_peers[0], z_peers[-1], y_peers[0], y_peers[-1]]
    for peer in near:
        pl.semaphore_signal(barrier, inc=1, device_id=peer, device_id_type=MESH)
    local = [
        pltpu.make_async_copy(source, target, local_sem.at[i])
        for i, (source, target) in enumerate(
            (
                (feat_hbm, feat_ref),
                (dst_hbm, keys.at[0]),
                (src_hbm, keys.at[1]),
                (ws_hbm, ws_ref),
                (wn_hbm, wn_ref),
                (cot_hbm, cot_ref),
                (tiles_hbm, tiles),
            )
        )
    ]
    for copy in local:
        copy.start()
    pl.semaphore_wait(barrier, len(near))

    def farther(ring, first):
        for i, peer in enumerate((ring[0], ring[-1])):
            pl.semaphore_signal(
                far_sem.at[first + i], inc=1, device_id=peer, device_id_type=MESH
            )

        def heard():
            for i in range(2):
                pl.semaphore_wait(far_sem.at[first + i], 1)

        return heard

    rounds = [(z_peers, 0)] * (Z_SIZE // 2 - 1) + [(y_peers, 2)] * (n_y // 2 - 1)
    rounds = [rounds[i] for i in sorted(range(len(rounds)), key=lambda i: rounds[:i].count(rounds[i]))]
    waiting = {}

    def next_round():
        if rounds:
            ring, first = rounds.pop(0)
            if first in waiting:
                waiting.pop(first)()
            waiting[first] = farther(ring, first)

    names, started = {}, []

    def send(name, src, dst, device):
        i = names.setdefault(name, len(names))
        copy = pltpu.make_async_remote_copy(
            src_ref=src,
            dst_ref=dst,
            send_sem=send_sem.at[i],
            recv_sem=recv_sem.at[i],
            device_id=device,
            device_id_type=MESH,
        )
        copy.start()
        started.append(copy)

    def arrive(name, dst):
        i = names[name]
        pltpu.make_async_remote_copy(
            src_ref=dst,
            dst_ref=dst,
            send_sem=send_sem.at[i],
            recv_sem=recv_sem.at[i],
            device_id=sib,
            device_id_type=MESH,
        ).wait_recv()

    lo, hi = pl.ds(0, half), pl.ds(half, half)
    q0 = c + 2
    q1 = 4 - 3 * c
    qs = (c, c + 4)

    def at(q, helper, a):
        return band.at[q * 8 + helper * 2 + a]

    def pair(q, helper):
        return band.at[pl.ds(q * 8 + helper * 2, 2)]

    fa, fb = feat_hbm.at[0], feat_hbm.at[1]
    send("a_r", fa, at(q0, h, 0), right)
    send("a_l", fa, at(q0, h, 0), left)
    send("b_n", fb, at(qs[0], h, 1), znext)
    send("b_p", fb, at(qs[1], h, 1), zprev)
    send("b_r", fb, at(q0, h, 1), right)
    send("b_l", fb, at(q0, h, 1), left)
    send("a_n", fa, at(qs[0], h, 0), znext)
    send("a_p", fa, at(qs[1], h, 0), zprev)
    send("s_own", feat_hbm, pair(q0, h), sib)
    next_round()
    next_round()
    local[0].wait()
    band[q0 * 8 + h * 2] = feat_ref[0]
    band[q0 * 8 + h * 2 + 1] = feat_ref[1]
    for copy in local[1:3]:
        copy.wait()
    write_order(keys, order_v, n_tiles)
    order = pltpu.make_async_copy(order_v, idx, local_sem.at[7])
    order.start()

    arrive("a_r", at(q0, hl, 0))
    send("a_rr", at(q0, hl, 0).at[lo], at(q0, hl, 0).at[lo], right)
    send("al_n", at(q0, hl, 0), at(qs[0], hl, 0), znext)
    send("al_p", at(q0, hl, 0), at(qs[1], hl, 0), zprev)
    arrive("a_l", at(q0, hr, 0))
    send("a_ll", at(q0, hr, 0).at[hi], at(q0, hr, 0).at[hi], left)
    send("ar_n", at(q0, hr, 0), at(qs[0], hr, 0), znext)
    send("ar_p", at(q0, hr, 0), at(qs[1], hr, 0), zprev)
    arrive("b_n", at(qs[0], h, 1))
    send("bn_r", at(qs[0], h, 1), at(qs[0], h, 1), right)
    send("bn_l", at(qs[0], h, 1), at(qs[0], h, 1), left)
    arrive("b_p", at(qs[1], h, 1))
    send("bp_r", at(qs[1], h, 1), at(qs[1], h, 1), right)
    send("bp_l", at(qs[1], h, 1), at(qs[1], h, 1), left)
    arrive("b_r", at(q0, hl, 1))
    send("b_rr", at(q0, hl, 1).at[lo], at(q0, hl, 1).at[lo], right)
    send("s_l", pair(q0, hl), pair(q0, hl), sib)
    arrive("b_l", at(q0, hr, 1))
    send("b_ll", at(q0, hr, 1).at[hi], at(q0, hr, 1).at[hi], left)
    send("s_r", pair(q0, hr), pair(q0, hr), sib)
    arrive("a_rr", at(q0, ho, 0).at[lo])
    arrive("a_ll", at(q0, ho, 0).at[hi])
    send("ao_n", at(q0, ho, 0), at(qs[0], ho, 0), znext)
    send("ao_p", at(q0, ho, 0), at(qs[1], ho, 0), zprev)
    arrive("bn_r", at(qs[0], hl, 1))
    send("bn_rr", at(qs[0], hl, 1).at[lo], at(qs[0], hl, 1).at[lo], right)
    arrive("bn_l", at(qs[0], hr, 1))
    send("bn_ll", at(qs[0], hr, 1).at[hi], at(qs[0], hr, 1).at[hi], left)
    arrive("bp_r", at(qs[1], hl, 1))
    send("bp_rr", at(qs[1], hl, 1).at[lo], at(qs[1], hl, 1).at[lo], right)
    next_round()
    next_round()
    arrive("bp_l", at(qs[1], hr, 1))
    send("bp_ll", at(qs[1], hr, 1).at[hi], at(qs[1], hr, 1).at[hi], left)
    arrive("a_n", at(qs[0], h, 0))
    arrive("a_p", at(qs[1], h, 0))
    send("t_own", pair(q1, h), pair(q1, h), sib)
    for copy in local[3:]:
        copy.wait()
    order.wait()
    rows, width = 2 * blk, feat_ref.shape[2]
    feats = feat_ref[...].reshape(rows, width)
    own_pre[...] = jnp.dot(feats, ws_ref[...], preferred_element_type=F32)
    arrive("b_rr", at(q0, ho, 1).at[lo])
    arrive("b_ll", at(q0, ho, 1).at[hi])
    send("s_o", pair(q0, ho), pair(q0, ho), sib)
    arrive("al_n", at(qs[0], hl, 0))
    arrive("al_p", at(qs[1], hl, 0))
    send("t_l", pair(q1, hl), pair(q1, hl), sib)
    arrive("ar_n", at(qs[0], hr, 0))
    arrive("ar_p", at(qs[1], hr, 0))
    send("t_r", pair(q1, hr), pair(q1, hr), sib)
    arrive("bn_rr", at(qs[0], ho, 1).at[lo])
    arrive("bn_ll", at(qs[0], ho, 1).at[hi])
    arrive("bp_rr", at(qs[1], ho, 1).at[lo])
    arrive("bp_ll", at(qs[1], ho, 1).at[hi])
    next_round()
    next_round()
    arrive("ao_n", at(qs[0], ho, 0))
    arrive("ao_p", at(qs[1], ho, 0))
    send("t_o", pair(q1, ho), pair(q1, ho), sib)
    p0, p1 = 3 - c, 1 + 3 * c
    for name, q, helper in (
        ("s_own", p0, h),
        ("s_l", p0, hl),
        ("s_r", p0, hr),
        ("t_own", p1, h),
        ("s_o", p0, ho),
        ("t_l", p1, hl),
        ("t_r", p1, hr),
        ("t_o", p1, ho),
    ):
        arrive(name, pair(q, helper))

    def forward(step, total):
        for u in range(UNROLL):
            i = step * UNROLL + u
            t = idx[0, i]
            s = idx[1, i] + 8 * c
            product = jnp.dot(tiles[t], band[s], preferred_element_type=F32)
            total = product + jnp.where(idx[2, i] > 0, total, 0.0)
            prods[i] = total.astype(BF16)
        return total

    zero = jnp.zeros((blk, band.shape[2]), F32)
    lax.fori_loop(0, n_tiles // UNROLL, forward, zero)

    def block_of(way, b):
        return jnp.where(idx[way + 4, b] > 0, prods[idx[way + 3, b]], jnp.zeros((), BF16))

    def owner_blocks(helper):
        for a in range(2):
            part[helper * 2 + a] = block_of(0, helper * 2 + a)

    waiting.pop(2)()
    next_round()
    owner_blocks(ho)
    send("p_rr", part.at[ho * 2], relay.at[0], right)
    send("p_ll", part.at[ho * 2 + 1], relay.at[1], left)
    owner_blocks(hr)
    send("p_r1", part.at[hr * 2 + 1], part_in.at[0, 1], right)
    owner_blocks(hl)
    send("p_l0", part.at[hl * 2], part_in.at[1, 0], left)
    owner_blocks(h)
    arrive("p_rr", relay.at[0])
    part[hr * 2] = (part[hr * 2].astype(F32) + relay[0].astype(F32)).astype(BF16)
    send("p_r0", part.at[hr * 2], part_in.at[0, 0], right)
    arrive("p_ll", relay.at[1])
    part[hl * 2 + 1] = (part[hl * 2 + 1].astype(F32) + relay[1].astype(F32)).astype(BF16)
    send("p_l1", part.at[hl * 2 + 1], part_in.at[1, 1], left)
    next_round()
    arrive("p_r1", part_in.at[0, 1])
    arrive("p_l0", part_in.at[1, 0])
    arrive("p_r0", part_in.at[0, 0])
    arrive("p_l1", part_in.at[1, 1])
    summed = part[pl.ds(h * 2, 2)].astype(F32) + part_in[0].astype(F32) + part_in[1].astype(F32)
    aggregate = summed.astype(BF16).reshape(rows, width)

    pre = own_pre[...] + jnp.dot(aggregate, wn_ref[...], preferred_element_type=F32)
    squash = jax.nn.sigmoid(pre)
    slope = squash * (1.0 + pre * (1.0 - squash))
    grad_pre = (cot_ref[...].astype(F32) * slope).astype(BF16)
    over_rows = (((0,), (0,)), ((), ()))
    for which in (1 - c, c):
        left_rows = jnp.where(which == 0, feats, aggregate)
        term = lax.dot_general(left_rows, grad_pre, over_rows, preferred_element_type=F32)
        if which is c:
            mats[...] = term
        else:
            mats_out[...] = term.astype(BF16)
            send("w_sib", mats_out, ar_sib, sib)
    dest_grad = lax.dot_general(
        grad_pre, wn_ref[...], (((1,), (1,)), ((), ())), preferred_element_type=F32
    ).astype(BF16)
    dest[pl.ds(h * 2, 2)] = dest_grad.reshape(2, blk, width)

    def dest_at(helper, a):
        return dest.at[helper * 2 + a]

    for a in range(2):
        send(f"d_r{a}", dest_at(h, a), dest_at(h, a), right)
        send(f"d_l{a}", dest_at(h, 1 - a), dest_at(h, 1 - a), left)
    hid_ref[...] = (pre * squash).astype(BF16)
    results = [(hid_ref, hid_hbm), (gf_ref, gf_hbm)]
    results += [(gw_ref.at[which], gw_hbm.at[which]) for which in (c, 1 - c)]
    results = [pltpu.make_async_copy(*pair, local_sem.at[8 + i]) for i, pair in enumerate(results)]
    results[0].start()
    assert not rounds
    for heard in waiting.values():
        heard()
    arrive("w_sib", ar_sib)
    summed = mats[...] + ar_sib[...].astype(F32)
    chunk_rows, chunk_cols = ar_x.shape[2:]
    quarter = summed.shape[0] // HELP
    for i in range(HELP):
        for j in range(n_y):
            r, s = i * quarter + j // 2 * chunk_rows, j % 2 * chunk_cols
            ar_x[i, j] = summed[r : r + chunk_rows, s : s + chunk_cols].astype(BF16)
    for n, (i, j) in enumerate(xy_steps):
        send(f"w_{i}_{j}", ar_x.at[(h + i) % HELP, (y + j) % n_y], ar_xin.at[n], xy_peer(i, j))
    arrive("d_r0", dest_at(hl, 0))
    send("d_rr", dest_at(hl, 0), dest_at(hl, 0), right)
    arrive("d_l0", dest_at(hr, 1))
    send("d_ll", dest_at(hr, 1), dest_at(hr, 1), left)
    gf_ref[...] = lax.dot_general(
        grad_pre, ws_ref[...], (((1,), (1,)), ((), ())), preferred_element_type=F32
    )
    arrive("d_r1", dest_at(hl, 1))
    arrive("d_l1", dest_at(hr, 0))
    arrive("d_rr", dest_at(ho, 0))
    arrive("d_ll", dest_at(ho, 1))

    def backward(step, total):
        for u in range(UNROLL):
            i = step * UNROLL + u
            t = idx[8, i]
            s = idx[9, i]
            product = lax.dot_general(
                tiles[t], dest[s], over_rows, preferred_element_type=F32
            )
            total = product + jnp.where(idx[10, i] > 0, total, 0.0)
            prods[i] = total.astype(BF16)
        return total

    steps = n_tiles // UNROLL
    total = lax.fori_loop(0, steps * 2 // 3, backward, zero)
    for n, (i, j) in reversed(list(enumerate(xy_steps))):
        arrive(f"w_{i}_{j}", ar_xin.at[n])
    chunk = ar_x[h, y].astype(F32) + jnp.sum(ar_xin[...].astype(F32), axis=0)
    ar_z[z] = chunk.astype(BF16)
    for j in z_steps:
        send(f"w_z{j}", ar_z.at[z], ar_z.at[z], z_peers[j - 1])
    lax.fori_loop(steps * 2 // 3, steps, backward, total)

    SOLO, MID, OTH = 0, 1, 2
    base = (32 * c, 16, 32 - 32 * c)
    sib_base = (None, 8 * (3 - 2 * c), 8 * (2 * c + 1))
    to = (((d + n_dom - 2 + 4 * c) % n_dom, h), None, ((d + n_dom + 2 - 4 * c) % n_dom, h))

    def pass_over(kind, a):
        def body(helper, carry):
            sib_out[kind - 1, a, helper] = block_of(8, sib_base[kind] + helper * 2 + a)
            return carry

        lax.fori_loop(0, HELP, body, 0)
        send(f"e_{kind}{a}", sib_out.at[kind - 1, a], sib_in.at[kind - 1, a], sib)

    def take(kind, a):
        if kind != SOLO:
            arrive(f"e_{kind}{a}", sib_in.at[kind - 1, a])

        def body(helper, carry):
            mine = block_of(8, base[kind] + helper * 2 + a)
            if kind != SOLO:
                mine = (mine.astype(F32) + sib_in[kind - 1, a, helper].astype(F32)).astype(BF16)
            g[kind, a, helper] = mine
            return carry

        lax.fori_loop(0, HELP, body, 0)
        if a == 1:
            send(f"rb_r{kind}", g.at[kind, 1, ho].at[lo], rb_in.at[0, kind], right)
            send(f"rb_l{kind}", g.at[kind, 1, ho].at[hi], rb_in.at[1, kind], left)
        elif kind != MID:
            for i, helper in enumerate((ho, hr, hl, h)):
                send(f"za_{kind}{i}", g.at[kind, 0, helper], za_in.at[kind // 2, i], to[kind])

    def pass_on(kind):
        arrive(f"rb_r{kind}", rb_in.at[0, kind])
        g[kind, 1, hr, lo] = (g[kind, 1, hr, lo].astype(F32) + rb_in[0, kind].astype(F32)).astype(BF16)
        send(f"fb_r{kind}", g.at[kind, 1, hr], fb_in.at[0, kind], right)
        arrive(f"rb_l{kind}", rb_in.at[1, kind])
        g[kind, 1, hl, hi] = (g[kind, 1, hl, hi].astype(F32) + rb_in[1, kind].astype(F32)).astype(BF16)
        send(f"fb_l{kind}", g.at[kind, 1, hl], fb_in.at[1, kind], left)

    def finish(kind):
        arrive(f"fb_r{kind}", fb_in.at[0, kind])
        arrive(f"fb_l{kind}", fb_in.at[1, kind])
        total = g[kind, 1, h].astype(F32) + fb_in[0, kind].astype(F32) + fb_in[1, kind].astype(F32)
        if kind == MID:
            gf_ref[pl.ds(blk, blk)] += total
        else:
            zb_out[kind // 2] = total.astype(BF16)
            send(f"zb_{kind}", zb_out.at[kind // 2], zb_in.at[kind // 2], to[kind])

    def add_z(i, helper):
        arrive(f"za_{SOLO}{i}", za_in.at[0, i])
        arrive(f"za_{OTH}{i}", za_in.at[1, i])
        total = g[MID, 0, helper].astype(F32) + za_in[0, i].astype(F32) + za_in[1, i].astype(F32)
        g[MID, 0, helper] = total.astype(BF16)

    pass_over(OTH, 1)
    pass_over(OTH, 0)
    take(SOLO, 1)
    take(SOLO, 0)
    pass_over(MID, 1)
    pass_over(MID, 0)
    take(OTH, 1)
    take(OTH, 0)
    take(MID, 1)
    pass_on(SOLO)
    take(MID, 0)
    for j in z_steps[::-1]:
        arrive(f"w_z{j}", ar_z.at[(z + Z_SIZE - j) % Z_SIZE])
    chunk = ar_z[0].astype(F32)
    for j in range(1, Z_SIZE):
        chunk = chunk + ar_z[j].astype(F32)
    ar_fin[c, h, y] = chunk.astype(BF16)
    for i, j in xy_steps:
        send(f"v_{i}_{j}", ar_fin.at[c, h, y], ar_fin.at[c, h, y], xy_peer(i, j))
    pass_on(OTH)
    pass_on(MID)
    finish(SOLO)
    add_z(0, ho)
    send("ra_r", g.at[MID, 0, ho].at[lo], ra_in.at[0], right)
    send("ra_l", g.at[MID, 0, ho].at[hi], ra_in.at[1], left)
    add_z(1, hr)
    add_z(2, hl)
    add_z(3, h)
    finish(OTH)
    arrive("ra_r", ra_in.at[0])
    g[MID, 0, hr, lo] = (g[MID, 0, hr, lo].astype(F32) + ra_in[0].astype(F32)).astype(BF16)
    send("fa_r", g.at[MID, 0, hr], fa_in.at[0], right)
    arrive("ra_l", ra_in.at[1])
    g[MID, 0, hl, hi] = (g[MID, 0, hl, hi].astype(F32) + ra_in[1].astype(F32)).astype(BF16)
    send("fa_l", g.at[MID, 0, hl], fa_in.at[1], left)

    finish(MID)
    for kind in (SOLO, OTH):
        arrive(f"zb_{kind}", zb_in.at[kind // 2])
        gf_ref[pl.ds(blk, blk)] += zb_in[kind // 2].astype(F32)
    arrive("fa_r", fa_in.at[0])
    arrive("fa_l", fa_in.at[1])
    gf_ref[pl.ds(0, blk)] += (
        g[MID, 0, h].astype(F32) + fa_in[0].astype(F32) + fa_in[1].astype(F32)
    )
    results[1].start()
    def write(which):
        for helper in range(HELP):
            for j in range(n_y):
                r, s = helper * quarter + j // 2 * chunk_rows, j % 2 * chunk_cols
                gw_ref[which, r : r + chunk_rows, s : s + chunk_cols] = ar_fin[
                    which, helper, j
                ].astype(F32)

    def all_sent():
        while started:
            started.pop(0).wait_send()

    all_sent()
    for i in (0, 1, 3, 2):
        helper = (h + HELP - i) % HELP
        for j in range(n_y):
            if i or j:
                arrive(f"v_{i}_{j}", ar_fin.at[c, helper, (y + n_y - j) % n_y])
        send(f"v_s{i}", ar_fin.at[c, helper], ar_fin.at[c, helper], sib)
    write(c)
    results[2].start()
    for i in range(HELP):
        arrive(f"v_s{i}", ar_fin.at[1 - c, (h + HELP - i) % HELP])
    write(1 - c)
    results[3].start()
    all_sent()
    for result in results:
        result.wait()
    assert len(names) == send_sem.shape[0]


def write_order(keys, order_v, n_tiles):
    shape = (n_tiles, order_v.shape[1])
    at = lax.broadcasted_iota(jnp.int32, shape, 0)
    lane = lax.broadcasted_iota(jnp.int32, shape, 1)
    tile = lane < n_tiles

    def column(row):
        return jnp.sum(jnp.where(at == lane, row, 0), axis=1, keepdims=True)

    rows = [jnp.broadcast_to(keys[i], (n_tiles, n_tiles)) for i in range(2)]
    pad = jnp.zeros((n_tiles, shape[1] - n_tiles), jnp.int32)
    rows = [jnp.concatenate([row, pad], axis=1) for row in rows]
    columns = [column(row) for row in rows]
    for way in range(2):
        row, key, other = rows[way], columns[way], columns[1 - way]
        tied = tile & (row == key) & (lane < at)
        before = tile & (row < key)
        rank = jnp.sum(jnp.where(tied | before, 1, 0), axis=1, keepdims=True)
        again = jnp.max(jnp.where(tied, 1, 0), axis=1, keepdims=True)
        here = rank == lane

        def total(values):
            return jnp.sum(values, axis=0, keepdims=True)

        results = (
            total(jnp.where(here, at, 0)),
            total(jnp.where(here, other, 0)),
            total(jnp.where(here, again, 0)),
            jnp.maximum(total(jnp.where(key <= lane, 1, 0)) - 1, 0),
            total(jnp.where(key == lane, 1, 0)),
        )
        for i, result in enumerate(results):
            order_v[pl.ds(way * 8 + i, 1), :] = result


def hand_over(*refs):
    sources, outs, held, sem = refs[:3], refs[3:7], refs[7:11], refs[11]
    sources = (*sources[:2], sources[2].at[0], sources[2].at[1])
    arrivals = [
        pltpu.make_async_copy(source, to, sem.at[i])
        for i, (source, to) in enumerate(zip(sources, held))
    ]
    leaving = [
        pltpu.make_async_copy(to, out, sem.at[4 + i])
        for i, (to, out) in enumerate(zip(held, outs))
    ]
    for copy in arrivals:
        copy.start()
    for arrival, copy in zip(arrivals, leaving):
        arrival.wait()
        copy.start()
    for copy in leaving:
        copy.wait()


def on_device(features, tile_vals, tile_dst, tile_src, w_self, w_neigh, cotangent):
    n_dom = lax.axis_size("dom")
    n_y = n_dom // (2 * Z_SIZE)
    rows, width = features.shape
    n_tiles, blk = tile_vals.shape[:2]
    quarter = width // HELP
    chunk = (n_y, quarter * 2 // n_y, width // 2)
    copies = 34 + 6 + 6 + 4 + 26 + 1 + HELP + 2 * (HELP * n_y - 1) + (Z_SIZE - 1)
    V = lambda *shape: pltpu.VMEM(shape, BF16)
    hbm = pl.BlockSpec(memory_space=pl.ANY)
    hidden, grad_features, grads = pl.pallas_call(
        functools.partial(kernel, n_dom),
        out_shape=(
            jax.ShapeDtypeStruct((rows, width), BF16),
            jax.ShapeDtypeStruct((rows, width), F32),
            jax.ShapeDtypeStruct((2, width, width), F32),
        ),
        in_specs=[hbm] * 7,
        out_specs=(hbm, hbm, hbm),
        scratch_shapes=[
            V(rows, width),
            pltpu.VMEM((rows, width), F32),
            pltpu.VMEM((2, width, width), F32),
            pltpu.VMEM((2, 1, n_tiles), jnp.int32),
            V(2, blk, width),
            V(width, width),
            V(width, width),
            V(rows, width),
            V(n_tiles, blk, blk),
            pltpu.VMEM((16, 128), jnp.int32),
            pltpu.SMEM((16, 128), jnp.int32),
            V(48, blk, width),
            V(n_tiles, blk, width),
            V(8, blk, width),
            V(2, blk, width),
            V(2, 2, blk, width),
            V(8, blk, width),
            pltpu.VMEM((width, width), F32),
            V(width, width),
            V(width, width),
            V(HELP, *chunk),
            V(HELP * n_y - 1, *chunk[1:]),
            V(Z_SIZE, *chunk[1:]),
            V(2, HELP, *chunk),
            V(2, 2, HELP, blk, width),
            V(2, 2, HELP, blk, width),
            V(3, 2, HELP, blk, width),
            V(2, 4, blk, width),
            V(2, 3, blk // 2, width),
            V(2, 3, blk, width),
            V(2, blk, width),
            V(2, blk, width),
            V(2, blk // 2, width),
            V(2, blk, width),
            pltpu.VMEM((rows, width), F32),
            pltpu.SemaphoreType.DMA((copies,)),
            pltpu.SemaphoreType.DMA((copies,)),
            pltpu.SemaphoreType.DMA((12,)),
            pltpu.SemaphoreType.REGULAR((4,)),
        ],
        compiler_params=pltpu.CompilerParams(
            collective_id=0, has_side_effects=True, vmem_limit_bytes=56 * 1024 * 1024
        ),
    )(
        tile_dst.reshape(1, n_tiles),
        tile_src.reshape(1, n_tiles),
        features.reshape(2, blk, width),
        tile_vals,
        w_self,
        w_neigh,
        cotangent,
    )
    shapes = (((rows, width), BF16), ((rows, width), F32), ((width, width), F32), ((width, width), F32))
    return pl.pallas_call(
        hand_over,
        out_shape=tuple(jax.ShapeDtypeStruct(*shape) for shape in shapes),
        in_specs=[hbm] * 3,
        out_specs=(hbm,) * 4,
        scratch_shapes=[
            *(pltpu.VMEM(*shape) for shape in shapes),
            pltpu.SemaphoreType.DMA((8,)),
        ],
    )(hidden, grad_features, grads)


def solution(mesh):
    in_specs = (
        P(("dom", "help"), None),
        P(("dom", "help"), None, None),
        P(("dom", "help")),
        P(("dom", "help")),
        P(),
        P(),
        P(("dom", "help"), None),
    )
    out_specs = (P(("dom", "help"), None), P(("dom", "help"), None), P(), P())
    return jax.shard_map(
        on_device, mesh=mesh, in_specs=in_specs, out_specs=out_specs, check_vma=False
    )
```

```python
import functools

import jax
import jax.numpy as jnp
from jax import lax
from jax.experimental import pallas as pl
from jax.experimental.pallas import tpu as pltpu
from jax.sharding import PartitionSpec as P

MESH = pl.DeviceIdType.MESH
F32, BF16 = jnp.float32, jnp.bfloat16
HELP = 4
Z_SIZE = 12
FORWARD_UNROLL, UNROLL = 24, 16


def kernel(
    n_dom,
    dst_hbm,
    src_hbm,
    feat_hbm,
    tiles_hbm,
    ws_hbm,
    wn_hbm,
    cot_hbm,
    hid_hbm,
    gf_hbm,
    gw_hbm,
    hid_ref,
    gf_ref,
    gw_ref,
    keys,
    feat_ref,
    ws_ref,
    wn_ref,
    cot_ref,
    tiles,
    order_v,
    idx,
    band,
    prods,
    part,
    relay,
    part_in,
    dest,
    mats,
    mats_out,
    ar_sib,
    ar_x,
    ar_xin,
    ar_z,
    ar_fin,
    sib_out,
    sib_in,
    g,
    za_in,
    rb_in,
    fb_in,
    zb_out,
    zb_in,
    ra_in,
    fa_in,
    own_pre,
    send_sem,
    recv_sem,
    local_sem,
    far_sem,
):
    n_y = n_dom // (2 * Z_SIZE)
    n_tiles, blk = tiles.shape[0], tiles.shape[1]
    half = blk // 2
    d, h = lax.axis_index("dom"), lax.axis_index("help")
    c, k = d % 2, d // 2
    z, y = k % Z_SIZE, k // Z_SIZE
    hr, hl, ho = (h + 1) % HELP, (h + 3) % HELP, (h + 2) % HELP

    sib = (d + 1 - 2 * c, h)
    right, left = (d, hr), (d, hl)

    def xy_peer(i, j):
        return ((((y + j) % n_y) * Z_SIZE + z) * 2 + c, (h + i) % HELP)

    znext, zprev = ((d + 2) % n_dom, h), ((d + n_dom - 2) % n_dom, h)
    y_peers = [xy_peer(0, j) for j in range(1, n_y)]
    def hops(steps, size):
        return min(steps, size - steps)

    xy_steps = [(i, j) for i in range(HELP) for j in range(n_y) if i or j]
    xy_steps.sort(key=lambda ij: -hops(ij[0], HELP) - hops(ij[1], n_y))
    z_steps = sorted(range(1, Z_SIZE), key=lambda j: -hops(j, Z_SIZE))
    z_peers = [((y * Z_SIZE + (z + j) % Z_SIZE) * 2 + c, h) for j in range(1, Z_SIZE)]

    barrier = pltpu.get_barrier_semaphore()
    near = [sib, right, left, znext, zprev, z_peers[0], z_peers[-1], y_peers[0], y_peers[-1]]
    for peer in near:
        pl.semaphore_signal(barrier, inc=1, device_id=peer, device_id_type=MESH)
    local = [
        pltpu.make_async_copy(source, target, local_sem.at[i])
        for i, (source, target) in enumerate(
            (
                (feat_hbm, feat_ref),
                (dst_hbm, keys.at[0]),
                (src_hbm, keys.at[1]),
                (ws_hbm, ws_ref),
                (wn_hbm, wn_ref),
                (cot_hbm, cot_ref),
                (tiles_hbm, tiles),
            )
        )
    ]
    for copy in local:
        copy.start()
    pl.semaphore_wait(barrier, len(near))

    def farther(ring, first):
        for i, peer in enumerate((ring[0], ring[-1])):
            pl.semaphore_signal(
                far_sem.at[first + i], inc=1, device_id=peer, device_id_type=MESH
            )

        def heard():
            for i in range(2):
                pl.semaphore_wait(far_sem.at[first + i], 1)

        return heard

    rounds = [(z_peers, 0)] * (Z_SIZE // 2 - 1) + [(y_peers, 2)] * (n_y // 2 - 1)
    rounds = [rounds[i] for i in sorted(range(len(rounds)), key=lambda i: rounds[:i].count(rounds[i]))]
    waiting = {}

    def next_round():
        if rounds:
            ring, first = rounds.pop(0)
            if first in waiting:
                waiting.pop(first)()
            waiting[first] = farther(ring, first)

    names, started = {}, []

    def send(name, src, dst, device):
        i = names.setdefault(name, len(names))
        copy = pltpu.make_async_remote_copy(
            src_ref=src,
            dst_ref=dst,
            send_sem=send_sem.at[i],
            recv_sem=recv_sem.at[i],
            device_id=device,
            device_id_type=MESH,
        )
        copy.start()
        started.append(copy)

    def arrive(name, dst):
        i = names[name]
        pltpu.make_async_remote_copy(
            src_ref=dst,
            dst_ref=dst,
            send_sem=send_sem.at[i],
            recv_sem=recv_sem.at[i],
            device_id=sib,
            device_id_type=MESH,
        ).wait_recv()

    lo, hi = pl.ds(0, half), pl.ds(half, half)
    q0 = c + 2
    q1 = 4 - 3 * c
    qs = (c, c + 4)

    def at(q, helper, a):
        return band.at[q * 8 + helper * 2 + a]

    def pair(q, helper):
        return band.at[pl.ds(q * 8 + helper * 2, 2)]

    fa, fb = feat_hbm.at[0], feat_hbm.at[1]
    send("a_r", fa, at(q0, h, 0), right)
    send("a_l", fa, at(q0, h, 0), left)
    send("b_n", fb, at(qs[0], h, 1), znext)
    send("b_p", fb, at(qs[1], h, 1), zprev)
    send("b_r", fb, at(q0, h, 1), right)
    send("b_l", fb, at(q0, h, 1), left)
    send("a_n", fa, at(qs[0], h, 0), znext)
    send("a_p", fa, at(qs[1], h, 0), zprev)
    send("s_own", feat_hbm, pair(q0, h), sib)
    next_round()
    next_round()
    local[0].wait()
    band[q0 * 8 + h * 2] = feat_ref[0]
    band[q0 * 8 + h * 2 + 1] = feat_ref[1]
    for copy in local[1:3]:
        copy.wait()
    write_order(keys, order_v, n_tiles)
    order = pltpu.make_async_copy(order_v, idx, local_sem.at[7])
    order.start()

    arrive("a_r", at(q0, hl, 0))
    send("a_rr", at(q0, hl, 0).at[lo], at(q0, hl, 0).at[lo], right)
    send("al_n", at(q0, hl, 0), at(qs[0], hl, 0), znext)
    send("al_p", at(q0, hl, 0), at(qs[1], hl, 0), zprev)
    arrive("a_l", at(q0, hr, 0))
    send("a_ll", at(q0, hr, 0).at[hi], at(q0, hr, 0).at[hi], left)
    send("ar_n", at(q0, hr, 0), at(qs[0], hr, 0), znext)
    send("ar_p", at(q0, hr, 0), at(qs[1], hr, 0), zprev)
    arrive("b_n", at(qs[0], h, 1))
    send("bn_r", at(qs[0], h, 1), at(qs[0], h, 1), right)
    send("bn_l", at(qs[0], h, 1), at(qs[0], h, 1), left)
    arrive("b_p", at(qs[1], h, 1))
    send("bp_r", at(qs[1], h, 1), at(qs[1], h, 1), right)
    send("bp_l", at(qs[1], h, 1), at(qs[1], h, 1), left)
    arrive("b_r", at(q0, hl, 1))
    send("b_rr", at(q0, hl, 1).at[lo], at(q0, hl, 1).at[lo], right)
    send("s_l", pair(q0, hl), pair(q0, hl), sib)
    arrive("b_l", at(q0, hr, 1))
    send("b_ll", at(q0, hr, 1).at[hi], at(q0, hr, 1).at[hi], left)
    send("s_r", pair(q0, hr), pair(q0, hr), sib)
    arrive("a_rr", at(q0, ho, 0).at[lo])
    arrive("a_ll", at(q0, ho, 0).at[hi])
    send("ao_n", at(q0, ho, 0), at(qs[0], ho, 0), znext)
    send("ao_p", at(q0, ho, 0), at(qs[1], ho, 0), zprev)
    arrive("bn_r", at(qs[0], hl, 1))
    send("bn_rr", at(qs[0], hl, 1).at[lo], at(qs[0], hl, 1).at[lo], right)
    arrive("bn_l", at(qs[0], hr, 1))
    send("bn_ll", at(qs[0], hr, 1).at[hi], at(qs[0], hr, 1).at[hi], left)
    arrive("bp_r", at(qs[1], hl, 1))
    send("bp_rr", at(qs[1], hl, 1).at[lo], at(qs[1], hl, 1).at[lo], right)
    next_round()
    next_round()
    arrive("bp_l", at(qs[1], hr, 1))
    send("bp_ll", at(qs[1], hr, 1).at[hi], at(qs[1], hr, 1).at[hi], left)
    arrive("a_n", at(qs[0], h, 0))
    arrive("a_p", at(qs[1], h, 0))
    send("t_own", pair(q1, h), pair(q1, h), sib)
    for copy in local[3:]:
        copy.wait()
    order.wait()
    rows, width = 2 * blk, feat_ref.shape[2]
    feats = feat_ref[...].reshape(rows, width)
    own_pre[...] = jnp.dot(feats, ws_ref[...], preferred_element_type=F32)
    arrive("b_rr", at(q0, ho, 1).at[lo])
    arrive("b_ll", at(q0, ho, 1).at[hi])
    send("s_o", pair(q0, ho), pair(q0, ho), sib)
    arrive("al_n", at(qs[0], hl, 0))
    arrive("al_p", at(qs[1], hl, 0))
    send("t_l", pair(q1, hl), pair(q1, hl), sib)
    arrive("ar_n", at(qs[0], hr, 0))
    arrive("ar_p", at(qs[1], hr, 0))
    send("t_r", pair(q1, hr), pair(q1, hr), sib)
    arrive("bn_rr", at(qs[0], ho, 1).at[lo])
    arrive("bn_ll", at(qs[0], ho, 1).at[hi])
    arrive("bp_rr", at(qs[1], ho, 1).at[lo])
    arrive("bp_ll", at(qs[1], ho, 1).at[hi])
    next_round()
    next_round()
    arrive("ao_n", at(qs[0], ho, 0))
    arrive("ao_p", at(qs[1], ho, 0))
    send("t_o", pair(q1, ho), pair(q1, ho), sib)
    p0, p1 = 3 - c, 1 + 3 * c
    for name, q, helper in (
        ("s_own", p0, h),
        ("s_l", p0, hl),
        ("s_r", p0, hr),
        ("t_own", p1, h),
        ("s_o", p0, ho),
        ("t_l", p1, hl),
        ("t_r", p1, hr),
        ("t_o", p1, ho),
    ):
        arrive(name, pair(q, helper))

    def forward(step, total):
        for u in range(FORWARD_UNROLL):
            i = step * FORWARD_UNROLL + u
            t = idx[0, i]
            s = idx[1, i] + 8 * c
            product = jnp.dot(tiles[t], band[s], preferred_element_type=F32)
            total = product + jnp.where(idx[2, i] > 0, total, 0.0)
            prods[i] = total.astype(BF16)
        return total

    zero = jnp.zeros((blk, band.shape[2]), F32)
    lax.fori_loop(0, n_tiles // FORWARD_UNROLL, forward, zero)

    def block_of(way, b):
        return jnp.where(idx[way + 4, b] > 0, prods[idx[way + 3, b]], jnp.zeros((), BF16))

    def owner_blocks(helper):
        for a in range(2):
            part[helper * 2 + a] = block_of(0, helper * 2 + a)

    waiting.pop(2)()
    next_round()
    owner_blocks(ho)
    send("p_rr", part.at[ho * 2], relay.at[0], right)
    send("p_ll", part.at[ho * 2 + 1], relay.at[1], left)
    owner_blocks(hr)
    send("p_r1", part.at[hr * 2 + 1], part_in.at[0, 1], right)
    owner_blocks(hl)
    send("p_l0", part.at[hl * 2], part_in.at[1, 0], left)
    owner_blocks(h)
    arrive("p_rr", relay.at[0])
    part[hr * 2] = (part[hr * 2].astype(F32) + relay[0].astype(F32)).astype(BF16)
    send("p_r0", part.at[hr * 2], part_in.at[0, 0], right)
    arrive("p_ll", relay.at[1])
    part[hl * 2 + 1] = (part[hl * 2 + 1].astype(F32) + relay[1].astype(F32)).astype(BF16)
    send("p_l1", part.at[hl * 2 + 1], part_in.at[1, 1], left)
    next_round()
    arrive("p_r1", part_in.at[0, 1])
    arrive("p_l0", part_in.at[1, 0])
    arrive("p_r0", part_in.at[0, 0])
    arrive("p_l1", part_in.at[1, 1])
    summed = part[pl.ds(h * 2, 2)].astype(F32) + part_in[0].astype(F32) + part_in[1].astype(F32)
    aggregate = summed.astype(BF16).reshape(rows, width)

    pre = own_pre[...] + jnp.dot(aggregate, wn_ref[...], preferred_element_type=F32)
    squash = jax.nn.sigmoid(pre)
    slope = squash * (1.0 + pre * (1.0 - squash))
    grad_pre = (cot_ref[...].astype(F32) * slope).astype(BF16)
    over_rows = (((0,), (0,)), ((), ()))
    for which in (1 - c, c):
        left_rows = jnp.where(which == 0, feats, aggregate)
        term = lax.dot_general(left_rows, grad_pre, over_rows, preferred_element_type=F32)
        if which is c:
            mats[...] = term
        else:
            mats_out[...] = term.astype(BF16)
            send("w_sib", mats_out, ar_sib, sib)
    dest_grad = lax.dot_general(
        grad_pre, wn_ref[...], (((1,), (1,)), ((), ())), preferred_element_type=F32
    ).astype(BF16)
    dest[pl.ds(h * 2, 2)] = dest_grad.reshape(2, blk, width)

    def dest_at(helper, a):
        return dest.at[helper * 2 + a]

    for a in range(2):
        send(f"d_r{a}", dest_at(h, a), dest_at(h, a), right)
        send(f"d_l{a}", dest_at(h, 1 - a), dest_at(h, 1 - a), left)
    hid_ref[...] = (pre * squash).astype(BF16)
    results = [(hid_ref, hid_hbm), (gf_ref, gf_hbm)]
    results += [(gw_ref.at[which], gw_hbm.at[which]) for which in (c, 1 - c)]
    results = [pltpu.make_async_copy(*pair, local_sem.at[8 + i]) for i, pair in enumerate(results)]
    results[0].start()
    assert not rounds
    for heard in waiting.values():
        heard()
    arrive("w_sib", ar_sib)
    summed = mats[...] + ar_sib[...].astype(F32)
    chunk_rows, chunk_cols = ar_x.shape[2:]
    quarter = summed.shape[0] // HELP
    for i in range(HELP):
        for j in range(n_y):
            r, s = i * quarter + j // 2 * chunk_rows, j % 2 * chunk_cols
            ar_x[i, j] = summed[r : r + chunk_rows, s : s + chunk_cols].astype(BF16)
    for n, (i, j) in enumerate(xy_steps):
        send(f"w_{i}_{j}", ar_x.at[(h + i) % HELP, (y + j) % n_y], ar_xin.at[n], xy_peer(i, j))
    arrive("d_r0", dest_at(hl, 0))
    send("d_rr", dest_at(hl, 0), dest_at(hl, 0), right)
    arrive("d_l0", dest_at(hr, 1))
    send("d_ll", dest_at(hr, 1), dest_at(hr, 1), left)
    gf_ref[...] = lax.dot_general(
        grad_pre, ws_ref[...], (((1,), (1,)), ((), ())), preferred_element_type=F32
    )
    arrive("d_r1", dest_at(hl, 1))
    arrive("d_l1", dest_at(hr, 0))
    arrive("d_rr", dest_at(ho, 0))
    arrive("d_ll", dest_at(ho, 1))

    def backward(step, total):
        for u in range(UNROLL):
            i = step * UNROLL + u
            t = idx[8, i]
            s = idx[9, i]
            product = lax.dot_general(
                tiles[t], dest[s], over_rows, preferred_element_type=F32
            )
            total = product + jnp.where(idx[10, i] > 0, total, 0.0)
            prods[i] = total.astype(BF16)
        return total

    steps = n_tiles // UNROLL
    total = lax.fori_loop(0, steps * 2 // 3, backward, zero)
    for n, (i, j) in reversed(list(enumerate(xy_steps))):
        arrive(f"w_{i}_{j}", ar_xin.at[n])
    chunk = ar_x[h, y].astype(F32) + jnp.sum(ar_xin[...].astype(F32), axis=0)
    ar_z[z] = chunk.astype(BF16)
    for j in z_steps:
        send(f"w_z{j}", ar_z.at[z], ar_z.at[z], z_peers[j - 1])
    lax.fori_loop(steps * 2 // 3, steps, backward, total)

    SOLO, MID, OTH = 0, 1, 2
    base = (32 * c, 16, 32 - 32 * c)
    sib_base = (None, 8 * (3 - 2 * c), 8 * (2 * c + 1))
    to = (((d + n_dom - 2 + 4 * c) % n_dom, h), None, ((d + n_dom + 2 - 4 * c) % n_dom, h))

    def pass_over(kind, a):
        def body(helper, carry):
            sib_out[kind - 1, a, helper] = block_of(8, sib_base[kind] + helper * 2 + a)
            return carry

        lax.fori_loop(0, HELP, body, 0)
        send(f"e_{kind}{a}", sib_out.at[kind - 1, a], sib_in.at[kind - 1, a], sib)

    def take(kind, a):
        if kind != SOLO:
            arrive(f"e_{kind}{a}", sib_in.at[kind - 1, a])

        def body(helper, carry):
            mine = block_of(8, base[kind] + helper * 2 + a)
            if kind != SOLO:
                mine = (mine.astype(F32) + sib_in[kind - 1, a, helper].astype(F32)).astype(BF16)
            g[kind, a, helper] = mine
            return carry

        lax.fori_loop(0, HELP, body, 0)
        if a == 1:
            send(f"rb_r{kind}", g.at[kind, 1, ho].at[lo], rb_in.at[0, kind], right)
            send(f"rb_l{kind}", g.at[kind, 1, ho].at[hi], rb_in.at[1, kind], left)
        elif kind != MID:
            for i, helper in enumerate((ho, hr, hl, h)):
                send(f"za_{kind}{i}", g.at[kind, 0, helper], za_in.at[kind // 2, i], to[kind])

    def pass_on(kind):
        arrive(f"rb_r{kind}", rb_in.at[0, kind])
        g[kind, 1, hr, lo] = (g[kind, 1, hr, lo].astype(F32) + rb_in[0, kind].astype(F32)).astype(BF16)
        send(f"fb_r{kind}", g.at[kind, 1, hr], fb_in.at[0, kind], right)
        arrive(f"rb_l{kind}", rb_in.at[1, kind])
        g[kind, 1, hl, hi] = (g[kind, 1, hl, hi].astype(F32) + rb_in[1, kind].astype(F32)).astype(BF16)
        send(f"fb_l{kind}", g.at[kind, 1, hl], fb_in.at[1, kind], left)

    def finish(kind):
        arrive(f"fb_r{kind}", fb_in.at[0, kind])
        arrive(f"fb_l{kind}", fb_in.at[1, kind])
        total = g[kind, 1, h].astype(F32) + fb_in[0, kind].astype(F32) + fb_in[1, kind].astype(F32)
        if kind == MID:
            gf_ref[pl.ds(blk, blk)] += total
        else:
            zb_out[kind // 2] = total.astype(BF16)
            send(f"zb_{kind}", zb_out.at[kind // 2], zb_in.at[kind // 2], to[kind])

    def add_z(i, helper):
        arrive(f"za_{SOLO}{i}", za_in.at[0, i])
        arrive(f"za_{OTH}{i}", za_in.at[1, i])
        total = g[MID, 0, helper].astype(F32) + za_in[0, i].astype(F32) + za_in[1, i].astype(F32)
        g[MID, 0, helper] = total.astype(BF16)

    pass_over(OTH, 1)
    pass_over(OTH, 0)
    take(SOLO, 1)
    take(SOLO, 0)
    pass_over(MID, 1)
    pass_over(MID, 0)
    take(OTH, 1)
    take(OTH, 0)
    take(MID, 1)
    pass_on(SOLO)
    take(MID, 0)
    for j in z_steps[::-1]:
        arrive(f"w_z{j}", ar_z.at[(z + Z_SIZE - j) % Z_SIZE])
    chunk = ar_z[0].astype(F32)
    for j in range(1, Z_SIZE):
        chunk = chunk + ar_z[j].astype(F32)
    ar_fin[c, h, y] = chunk.astype(BF16)
    for i, j in xy_steps:
        send(f"v_{i}_{j}", ar_fin.at[c, h, y], ar_fin.at[c, h, y], xy_peer(i, j))
    pass_on(OTH)
    pass_on(MID)
    finish(SOLO)
    add_z(0, ho)
    send("ra_r", g.at[MID, 0, ho].at[lo], ra_in.at[0], right)
    send("ra_l", g.at[MID, 0, ho].at[hi], ra_in.at[1], left)
    add_z(1, hr)
    add_z(2, hl)
    add_z(3, h)
    finish(OTH)
    arrive("ra_r", ra_in.at[0])
    g[MID, 0, hr, lo] = (g[MID, 0, hr, lo].astype(F32) + ra_in[0].astype(F32)).astype(BF16)
    send("fa_r", g.at[MID, 0, hr], fa_in.at[0], right)
    arrive("ra_l", ra_in.at[1])
    g[MID, 0, hl, hi] = (g[MID, 0, hl, hi].astype(F32) + ra_in[1].astype(F32)).astype(BF16)
    send("fa_l", g.at[MID, 0, hl], fa_in.at[1], left)

    finish(MID)
    for kind in (SOLO, OTH):
        arrive(f"zb_{kind}", zb_in.at[kind // 2])
        gf_ref[pl.ds(blk, blk)] += zb_in[kind // 2].astype(F32)
    arrive("fa_r", fa_in.at[0])
    arrive("fa_l", fa_in.at[1])
    gf_ref[pl.ds(0, blk)] += (
        g[MID, 0, h].astype(F32) + fa_in[0].astype(F32) + fa_in[1].astype(F32)
    )
    results[1].start()
    def write(which):
        for helper in range(HELP):
            for j in range(n_y):
                r, s = helper * quarter + j // 2 * chunk_rows, j % 2 * chunk_cols
                gw_ref[which, r : r + chunk_rows, s : s + chunk_cols] = ar_fin[
                    which, helper, j
                ].astype(F32)

    def all_sent():
        while started:
            started.pop(0).wait_send()

    all_sent()
    for i in (0, 1, 3, 2):
        helper = (h + HELP - i) % HELP
        for j in range(n_y):
            if i or j:
                arrive(f"v_{i}_{j}", ar_fin.at[c, helper, (y + n_y - j) % n_y])
        send(f"v_s{i}", ar_fin.at[c, helper], ar_fin.at[c, helper], sib)
    write(c)
    results[2].start()
    for i in range(HELP):
        arrive(f"v_s{i}", ar_fin.at[1 - c, (h + HELP - i) % HELP])
    write(1 - c)
    results[3].start()
    all_sent()
    for result in results:
        result.wait()
    assert len(names) == send_sem.shape[0]


def write_order(keys, order_v, n_tiles):
    shape = (n_tiles, order_v.shape[1])
    at = lax.broadcasted_iota(jnp.int32, shape, 0)
    lane = lax.broadcasted_iota(jnp.int32, shape, 1)
    tile = lane < n_tiles

    def column(row):
        return jnp.sum(jnp.where(at == lane, row, 0), axis=1, keepdims=True)

    rows = [jnp.broadcast_to(keys[i], (n_tiles, n_tiles)) for i in range(2)]
    pad = jnp.zeros((n_tiles, shape[1] - n_tiles), jnp.int32)
    rows = [jnp.concatenate([row, pad], axis=1) for row in rows]
    columns = [column(row) for row in rows]
    for way in range(2):
        row, key, other = rows[way], columns[way], columns[1 - way]
        tied = tile & (row == key) & (lane < at)
        before = tile & (row < key)
        rank = jnp.sum(jnp.where(tied | before, 1, 0), axis=1, keepdims=True)
        again = jnp.max(jnp.where(tied, 1, 0), axis=1, keepdims=True)
        here = rank == lane

        def total(values):
            return jnp.sum(values, axis=0, keepdims=True)

        results = (
            total(jnp.where(here, at, 0)),
            total(jnp.where(here, other, 0)),
            total(jnp.where(here, again, 0)),
            jnp.maximum(total(jnp.where(key <= lane, 1, 0)) - 1, 0),
            total(jnp.where(key == lane, 1, 0)),
        )
        for i, result in enumerate(results):
            order_v[pl.ds(way * 8 + i, 1), :] = result


def hand_over(*refs):
    sources, outs, held, sem = refs[:3], refs[3:7], refs[7:11], refs[11]
    sources = (*sources[:2], sources[2].at[0], sources[2].at[1])
    arrivals = [
        pltpu.make_async_copy(source, to, sem.at[i])
        for i, (source, to) in enumerate(zip(sources, held))
    ]
    leaving = [
        pltpu.make_async_copy(to, out, sem.at[4 + i])
        for i, (to, out) in enumerate(zip(held, outs))
    ]
    for copy in arrivals:
        copy.start()
    for arrival, copy in zip(arrivals, leaving):
        arrival.wait()
        copy.start()
    for copy in leaving:
        copy.wait()


def on_device(features, tile_vals, tile_dst, tile_src, w_self, w_neigh, cotangent):
    n_dom = lax.axis_size("dom")
    n_y = n_dom // (2 * Z_SIZE)
    rows, width = features.shape
    n_tiles, blk = tile_vals.shape[:2]
    quarter = width // HELP
    chunk = (n_y, quarter * 2 // n_y, width // 2)
    copies = 34 + 6 + 6 + 4 + 26 + 1 + HELP + 2 * (HELP * n_y - 1) + (Z_SIZE - 1)
    V = lambda *shape: pltpu.VMEM(shape, BF16)
    hbm = pl.BlockSpec(memory_space=pl.ANY)
    hidden, grad_features, grads = pl.pallas_call(
        functools.partial(kernel, n_dom),
        out_shape=(
            jax.ShapeDtypeStruct((rows, width), BF16),
            jax.ShapeDtypeStruct((rows, width), F32),
            jax.ShapeDtypeStruct((2, width, width), F32),
        ),
        in_specs=[hbm] * 7,
        out_specs=(hbm, hbm, hbm),
        scratch_shapes=[
            V(rows, width),
            pltpu.VMEM((rows, width), F32),
            pltpu.VMEM((2, width, width), F32),
            pltpu.VMEM((2, 1, n_tiles), jnp.int32),
            V(2, blk, width),
            V(width, width),
            V(width, width),
            V(rows, width),
            V(n_tiles, blk, blk),
            pltpu.VMEM((16, 128), jnp.int32),
            pltpu.SMEM((16, 128), jnp.int32),
            V(48, blk, width),
            V(n_tiles, blk, width),
            V(8, blk, width),
            V(2, blk, width),
            V(2, 2, blk, width),
            V(8, blk, width),
            pltpu.VMEM((width, width), F32),
            V(width, width),
            V(width, width),
            V(HELP, *chunk),
            V(HELP * n_y - 1, *chunk[1:]),
            V(Z_SIZE, *chunk[1:]),
            V(2, HELP, *chunk),
            V(2, 2, HELP, blk, width),
            V(2, 2, HELP, blk, width),
            V(3, 2, HELP, blk, width),
            V(2, 4, blk, width),
            V(2, 3, blk // 2, width),
            V(2, 3, blk, width),
            V(2, blk, width),
            V(2, blk, width),
            V(2, blk // 2, width),
            V(2, blk, width),
            pltpu.VMEM((rows, width), F32),
            pltpu.SemaphoreType.DMA((copies,)),
            pltpu.SemaphoreType.DMA((copies,)),
            pltpu.SemaphoreType.DMA((12,)),
            pltpu.SemaphoreType.REGULAR((4,)),
        ],
        compiler_params=pltpu.CompilerParams(
            collective_id=0, has_side_effects=True, vmem_limit_bytes=56 * 1024 * 1024
        ),
    )(
        tile_dst.reshape(1, n_tiles),
        tile_src.reshape(1, n_tiles),
        features.reshape(2, blk, width),
        tile_vals,
        w_self,
        w_neigh,
        cotangent,
    )
    shapes = (((rows, width), BF16), ((rows, width), F32), ((width, width), F32), ((width, width), F32))
    return pl.pallas_call(
        hand_over,
        out_shape=tuple(jax.ShapeDtypeStruct(*shape) for shape in shapes),
        in_specs=[hbm] * 3,
        out_specs=(hbm,) * 4,
        scratch_shapes=[
            *(pltpu.VMEM(*shape) for shape in shapes),
            pltpu.SemaphoreType.DMA((8,)),
        ],
    )(hidden, grad_features, grads)


def solution(mesh):
    in_specs = (
        P(("dom", "help"), None),
        P(("dom", "help"), None, None),
        P(("dom", "help")),
        P(("dom", "help")),
        P(),
        P(),
        P(("dom", "help"), None),
    )
    out_specs = (P(("dom", "help"), None), P(("dom", "help"), None), P(), P())
    return jax.shard_map(
        on_device, mesh=mesh, in_specs=in_specs, out_specs=out_specs, check_vma=False
    )
```
